32 devices in a mesh: groups: 2 (over y), tp: 8 (over z, x), rep: 2 (over core).
Axes of the slice: x: 2, y: 2, z: 4, core: 2. Of those that a mesh axis runs over, the one named last changes fastest.
Arguments:
- tokens: bfloat16 [8, 16384], P('groups', ('tp', 'rep')), parts along dimension 0, may hold values from -6 to 6
- query_matrix: bfloat16 [16384, 16384], P(('tp', 'rep')), may hold values from -0.0625 to 0.0625
- key_value_weight: bfloat16 [16384, 2048], P(('tp', 'rep')), may hold values from -0.046875 to 0.046875
- output_matrix: bfloat16 [16384, 16384], P(None, ('tp', 'rep')), may hold values from -0.1875 to 0.1875
- adapter_down_factors: bfloat16 [16384, 192], P(('tp', 'rep')), may hold values from -0.046875 to 0.046875
- adapter_up_factors: bfloat16 [64, 18432], P('tp'), may hold values from -0.1875 to 0.1875
- output_down_factor: bfloat16 [16384, 64], P(('tp', 'rep')), may hold values from -0.1875 to 0.1875
- output_up_factor: bfloat16 [64, 16384], P(None, ('tp', 'rep')), may hold values from -0.375 to 0.375
- rotated_key_cache: bfloat16 [64, 4096, 128], P(('groups', 'tp', 'rep')), parts along dimension 0, may hold values from -218 to 218
- cached_value_rows: bfloat16 [64, 4096, 128], P(('groups', 'tp', 'rep')), parts along dimension 0, may hold values from -6 to 6
- lengths: int32 [8], P('groups'), parts along dimension 0, may hold values from 1 to 4096, as said below
- positions: int32 [8], P('groups'), parts along dimension 0, may hold values from 0 to 8191
Outputs:
- attention_out: bfloat16 [8, 16384], P('groups', ('tp', 'rep')), parts along dimension 0
- fresh_key: bfloat16 [64, 128], P(('groups', 'tp', 'rep')), parts along dimension 0
- fresh_value: bfloat16 [64, 128], P(('groups', 'tp', 'rep')), parts along dimension 0
The draws below stay inside these ranges and needn't reach their ends.
There are 2 independent parts, one for each index of `groups`. The reference program is written for one: setup_inputs(seed, part) draws one part's arguments, and reference() takes and returns one part's arrays. A program takes and returns all parts, laid end to end along the dimension named above; an argument that names none is the same for every part. Nothing has to cross between parts.
Inputs may be any that keep to these rules, and one draw needn't show every extreme that they name: `lengths`: some row has exactly 4096 cached keys in every draw.
All inputs are finite; a program needn't handle non-finite values.
Results may differ from the reference program's by a relative error of at most 0.0098.
Values may be sent and summed in bfloat16 or wider, within the bound.
No kernel may reach another device: no remote copies, remote signals or barrier semaphores. Data moves between devices by JAX's collectives and lax.ppermute only.
A program may use at most 192 MiB of HBM per device.

```python
import math
import jax
import jax.numpy as jnp
from jax import lax

MODEL_WIDTH = 16384
QUERY_HEADS = 128
KEY_HEADS = 8
HEAD_WIDTH = 128
ADAPTER_RANK = 64
CACHE = 4096
BATCH = 4


def draw_lengths(key, part):
    key = jax.random.fold_in(key, 11)
    first_key, second_key = jax.random.split(key)
    drawn = jax.random.randint(first_key, (BATCH,), 1, CACHE + 1)
    longest = jax.random.randint(second_key, (), 0, BATCH)
    return jnp.where(jnp.arange(BATCH) == longest, CACHE, drawn).astype(jnp.int32)


def draw_rotated_key_cache(key, part):
    key = jax.random.fold_in(key, 23)
    first_key = jax.random.fold_in(key, 0)
    array_shape = (KEY_HEADS * BATCH, CACHE, HEAD_WIDTH)
    return jnp.clip(jax.random.normal(first_key, array_shape, jnp.float32), -6.0, 6.0).astype(jnp.bfloat16)


def place_ends(values, stream_key, least, top_value):
    place = [jax.random.randint(jax.random.fold_in(stream_key, axis), (), 0, length) for axis, length in enumerate(values.shape)]
    widest = values.shape.index(max(values.shape))
    neighbour = place[:widest] + [(place[widest] + 1) % values.shape[widest]] + place[widest + 1:]
    return values.at[tuple(place)].set(least).at[tuple(neighbour)].set(top_value)


def raised(values, own_key, source, target, shards_of, factor):
    owner, partner = [(jnp.arange(values.shape[axis_at]) // (values.shape[axis_at] // shards_of)).reshape([-1 if axis == axis_at else 1 for axis in range(values.ndim)]) for axis_at in (source, target)]
    chosen = jax.random.permutation(own_key, shards_of)[partner]
    strong = (owner == chosen) | (owner == (partner + shards_of // 2) % shards_of)
    return jnp.where(strong, factor * values, values)


def block_levels(stream_key, dims, cuts, smallest, high):
    def one(dim, parts):
        steps = jax.random.uniform(jax.random.fold_in(jax.random.fold_in(stream_key, 6), dim), (parts,), jnp.float32, smallest / len(cuts), high / len(cuts))
        return jnp.repeat(jnp.exp(steps), dims[dim] // parts).reshape((-1,) + (1,) * (len(dims) - dim - 1))

    level = one(*cuts[0])
    for cut in cuts[1:]:
        level = level * one(*cut)
    return level


def scatter_about(stream_key, extent, scale, limit, cuts=(), kind=jnp.bfloat16):
    result = jax.random.normal(stream_key, extent, jnp.float32) * scale
    if len(cuts) > 0:
        result = block_levels(stream_key, extent, cuts, -0.22, 0.18) * result
    return jnp.clip(result, min=-limit, max=limit).astype(kind)


def noise_with(rng, dims, scale, most, pieces, heavy, kind=jnp.bfloat16):
    entries = scale * jax.random.normal(rng, dims, jnp.float32)
    if pieces:
        entries = entries * block_levels(rng, dims, pieces, -0.22, 0.18)
    return jnp.clip(raised(entries, jax.random.fold_in(rng, 3), *heavy), -most, most).astype(kind)


def setup_inputs(seed: int = 0, part: int = 0) -> dict:
    keys = jax.random.split(jax.random.key(seed), 13)
    own_keys = jax.random.split(jax.random.fold_in(keys[12], part), 13)
    tokens = scatter_about(own_keys[0], (BATCH, MODEL_WIDTH), 1.0, 6.0, ((1, 16),))
    query_matrix = noise_with(keys[1], (MODEL_WIDTH, QUERY_HEADS * HEAD_WIDTH), MODEL_WIDTH ** -0.5, 0.0625, ((0, 16),), (0, 1, 16, 2.0))
    key_value_weight = scatter_about(keys[2], (MODEL_WIDTH, 2 * KEY_HEADS * HEAD_WIDTH), MODEL_WIDTH ** -0.5, 0.046875, ((0, 16),))
    output_matrix = scatter_about(keys[3], (QUERY_HEADS * HEAD_WIDTH, MODEL_WIDTH), (QUERY_HEADS * HEAD_WIDTH // 16) ** -0.5, 0.1875, ((1, 16),))
    adapter_down_factors = scatter_about(keys[4], (MODEL_WIDTH, 3 * ADAPTER_RANK), MODEL_WIDTH ** -0.5, 0.046875, ((0, 16),))
    adapter_up_factors = scatter_about(keys[5], (ADAPTER_RANK, (QUERY_HEADS + 2 * KEY_HEADS) * HEAD_WIDTH), (16 * ADAPTER_RANK) ** -0.5, 0.1875, ((0, 8),))
    output_down_factor = scatter_about(keys[6], (QUERY_HEADS * HEAD_WIDTH, ADAPTER_RANK), (QUERY_HEADS * HEAD_WIDTH // 16) ** -0.5, 0.1875, ((0, 16),))
    output_up_factor = scatter_about(keys[7], (ADAPTER_RANK, MODEL_WIDTH), (4 * ADAPTER_RANK) ** -0.5, 0.375, ((1, 16),))
    rotated_key_cache = draw_rotated_key_cache(jax.random.fold_in(jax.random.fold_in(keys[12], part), 71), part)
    cached_value_rows = scatter_about(own_keys[9], (KEY_HEADS * BATCH, CACHE, HEAD_WIDTH), 1.0, 6.0, ((0, 16),))
    lengths = draw_lengths(jax.random.fold_in(jax.random.fold_in(keys[12], part), 71), part)
    positions = place_ends(jax.random.randint(own_keys[11], (BATCH,), 0, 2 * CACHE), jax.random.fold_in(own_keys[11], 1), 0, (2 * CACHE) - 1).astype(jnp.int32)
    return dict(tokens=tokens, query_matrix=query_matrix, key_value_weight=key_value_weight, output_matrix=output_matrix, adapter_down_factors=adapter_down_factors, adapter_up_factors=adapter_up_factors, output_down_factor=output_down_factor, output_up_factor=output_up_factor, rotated_key_cache=rotated_key_cache, cached_value_rows=cached_value_rows, lengths=lengths, positions=positions)


adapter_scale = 2.0
rope_base = 500000.0

def rope_angles(positions, head_size):
    half_size = head_size // 2
    frequency = jnp.power(rope_base, -2.0 * jnp.arange(half_size, dtype=jnp.float32) / head_size)
    return positions.astype(jnp.float32)[:, None] * frequency[None, :]

def rotate(field, angles):
    half_size = field.shape[-1] // 2
    cosine = jnp.cos(angles)[:, None, :]
    sine_part = jnp.sin(angles)[:, None, :]
    former = field[..., :half_size]
    latter = field[..., half_size:]
    return jnp.concatenate([former * cosine - latter * sine_part, latter * cosine + former * sine_part], axis=-1)

def attend(queries, new_key, new_value, key_rows, value_rows, lengths):
    scale_factor = 1.0 / math.sqrt(queries.shape[-1])
    query_wide = queries.astype(jnp.float32)
    scores = jnp.einsum('ngd,ncd->ngc', query_wide, key_rows.astype(jnp.float32)) * scale_factor
    own_score = jnp.einsum('ngd,nd->ng', query_wide, new_key.astype(jnp.float32)) * scale_factor
    in_range = jnp.arange(key_rows.shape[1], dtype=jnp.int32)[None, None, :] < lengths[:, None, None]
    scores = jnp.where(in_range, scores, -jnp.inf)
    highest = jnp.maximum(lax.optimization_barrier(jnp.max(scores, axis=-1)), own_score)
    weights = jnp.exp(scores - highest[..., None])
    own_weight = jnp.exp(own_score - highest)
    denominator = lax.optimization_barrier(jnp.sum(weights, axis=-1)) + own_weight
    prob_weights = (weights / denominator[..., None]).astype(jnp.bfloat16)
    own_prob = (own_weight / denominator).astype(jnp.bfloat16)
    mixture = jnp.einsum('ngc,ncd->ngd', prob_weights.astype(jnp.float32), value_rows.astype(jnp.float32))
    mixture = mixture + own_prob.astype(jnp.float32)[..., None] * new_value.astype(jnp.float32)[:, None, :]
    return mixture.astype(jnp.bfloat16)

def reference(tokens, query_matrix, key_value_weight, output_matrix, adapter_down_factors, adapter_up_factors, output_down_factor, output_up_factor, rotated_key_cache, cached_value_rows, lengths, positions):
    query_columns = QUERY_HEADS * HEAD_WIDTH
    key_value_columns = KEY_HEADS * HEAD_WIDTH
    group_heads = QUERY_HEADS // KEY_HEADS
    rank_row_block = jnp.dot(tokens, adapter_down_factors, preferred_element_type=jnp.float32).astype(jnp.bfloat16)
    query_linear = jnp.dot(tokens, query_matrix, preferred_element_type=jnp.float32)
    query_linear = query_linear + adapter_scale * jnp.dot(rank_row_block[:, :ADAPTER_RANK], adapter_up_factors[:, :query_columns], preferred_element_type=jnp.float32)
    key_value_linear = jnp.dot(tokens, key_value_weight, preferred_element_type=jnp.float32)
    key_linear = key_value_linear[:, :key_value_columns] + adapter_scale * jnp.dot(rank_row_block[:, ADAPTER_RANK:2 * ADAPTER_RANK], adapter_up_factors[:, query_columns:query_columns + key_value_columns], preferred_element_type=jnp.float32)
    value_linear = key_value_linear[:, key_value_columns:] + adapter_scale * jnp.dot(rank_row_block[:, 2 * ADAPTER_RANK:], adapter_up_factors[:, query_columns + key_value_columns:], preferred_element_type=jnp.float32)
    angles = rope_angles(positions, HEAD_WIDTH)
    queries = rotate(query_linear.reshape(BATCH, QUERY_HEADS, HEAD_WIDTH), angles).astype(jnp.bfloat16)
    fresh_key = rotate(key_linear.reshape(BATCH, KEY_HEADS, HEAD_WIDTH), angles).astype(jnp.bfloat16)
    fresh_value = value_linear.reshape(BATCH, KEY_HEADS, HEAD_WIDTH).astype(jnp.bfloat16)
    per_head = (queries.reshape(BATCH, KEY_HEADS, group_heads, HEAD_WIDTH).transpose(1, 0, 2, 3), fresh_key.transpose(1, 0, 2), fresh_value.transpose(1, 0, 2), rotated_key_cache.reshape(KEY_HEADS, BATCH, CACHE, HEAD_WIDTH), cached_value_rows.reshape(KEY_HEADS, BATCH, CACHE, HEAD_WIDTH))

    def one_head(items):
        return attend(items[0], items[1], items[2], items[3], items[4], lengths)
    mixture = lax.map(one_head, per_head)
    mixed_all = mixture.transpose(1, 0, 2, 3).reshape(BATCH, query_columns)
    low_rank_output = jnp.dot(mixed_all, output_down_factor, preferred_element_type=jnp.float32).astype(jnp.bfloat16)
    final_output = jnp.dot(mixed_all, output_matrix, preferred_element_type=jnp.float32)
    final_output = final_output + adapter_scale * jnp.dot(low_rank_output, output_up_factor, preferred_element_type=jnp.float32)
    key_out = fresh_key.transpose(1, 0, 2).reshape(KEY_HEADS * BATCH, HEAD_WIDTH)
    value_out = fresh_value.transpose(1, 0, 2).reshape(KEY_HEADS * BATCH, HEAD_WIDTH)
    return (final_output.astype(jnp.bfloat16), key_out, value_out)
```

```python
import math

import jax
import jax.numpy as jnp
from jax import lax
from jax.sharding import PartitionSpec as P

QUERY_HEADS = 128
KEY_HEADS = 8


adapter_scale = 2.0
rope_base = 500000.0


def rope_angles(positions, head_size):
    half_size = head_size // 2
    frequency = jnp.power(rope_base, -2.0 * jnp.arange(half_size, dtype=jnp.float32) / head_size)
    return positions.astype(jnp.float32)[:, None] * frequency[None, :]


def rotate(field, angles):
    half_size = field.shape[-1] // 2
    cosine = jnp.cos(angles)[:, None, :]
    sine_part = jnp.sin(angles)[:, None, :]
    former = field[..., :half_size]
    latter = field[..., half_size:]
    return jnp.concatenate(
        [former * cosine - latter * sine_part, latter * cosine + former * sine_part], axis=-1
    )


def attend(queries, new_key, new_value, key_rows, value_rows, lengths):
    scale_factor = 1.0 / math.sqrt(queries.shape[-1])
    scores = (
        jnp.einsum("ngd,ncd->ngc", queries, key_rows, preferred_element_type=jnp.float32)
        * scale_factor
    )
    own_score = (
        jnp.einsum("ngd,nd->ng", queries, new_key, preferred_element_type=jnp.float32)
        * scale_factor
    )
    in_range = (
        jnp.arange(key_rows.shape[1], dtype=jnp.int32)[None, None, :] < lengths[:, None, None]
    )
    scores = jnp.where(in_range, scores, -jnp.inf)
    highest = jnp.maximum(jnp.max(scores, axis=-1), own_score)
    weights = jnp.exp(scores - highest[..., None])
    own_weight = jnp.exp(own_score - highest)
    denominator = jnp.sum(weights, axis=-1) + own_weight
    prob_weights = (weights / denominator[..., None]).astype(jnp.bfloat16)
    own_prob = (own_weight / denominator).astype(jnp.bfloat16)
    mixture = jnp.einsum(
        "ngc,ncd->ngd", prob_weights, value_rows, preferred_element_type=jnp.float32
    )
    mixture = (
        mixture
        + own_prob.astype(jnp.float32)[..., None] * new_value.astype(jnp.float32)[:, None, :]
    )
    return mixture.astype(jnp.bfloat16)


def by_key_head(columns, head_size):
    rows = columns.shape[0]
    query_columns = QUERY_HEADS * head_size
    key_columns = KEY_HEADS * head_size
    query = columns[:, :query_columns].reshape(rows, KEY_HEADS, -1)
    key = columns[:, query_columns : query_columns + key_columns].reshape(rows, KEY_HEADS, -1)
    value = columns[:, query_columns + key_columns :].reshape(rows, KEY_HEADS, -1)
    return jnp.concatenate([query, key, value], axis=-1).transpose(1, 0, 2)


def gather_direct(value, devices, dev_index):
    pieces = [value]
    for step in range(1, devices):
        pairs = [(source, (source + step) % devices) for source in range(devices)]
        pieces.append(lax.ppermute(value, ("tp", "rep"), pairs))
    stacked = jnp.concatenate(pieces[::-1], axis=0)
    return jnp.roll(stacked, dev_index + 1, axis=0)


def per_device(
    tokens,
    query_matrix,
    key_value_weight,
    output_matrix,
    adapter_down_factors,
    adapter_up_factors,
    output_down_factor,
    output_up_factor,
    rotated_key_cache,
    cached_value_rows,
    lengths,
    positions,
):
    tp_count = lax.axis_size("tp")
    rep_count = lax.axis_size("rep")
    devices = tp_count * rep_count
    dev_index = lax.axis_index("tp") * rep_count + lax.axis_index("rep")
    head_size = rotated_key_cache.shape[2]
    row_count = rotated_key_cache.shape[0]
    batch_rows = tokens.shape[0]
    group_heads = QUERY_HEADS // KEY_HEADS
    blocks = devices // KEY_HEADS
    row_block = dev_index % blocks
    rank_width = adapter_down_factors.shape[1] // 3
    query_columns = QUERY_HEADS * head_size
    group_columns = group_heads * head_size
    block_cols = (group_heads + 2) * head_size

    up_parts = by_key_head(adapter_up_factors, head_size)
    up_parts = jnp.repeat(up_parts, tp_count // KEY_HEADS, axis=0)
    up_factor = lax.all_to_all(up_parts, "tp", split_axis=0, concat_axis=0, tiled=True)
    up_factor = up_factor.reshape(-1, block_cols)

    down_parts = [output_down_factor]
    for step in range(1, blocks):
        pairs = [
            (source, source // blocks * blocks + (source + step) % blocks)
            for source in range(devices)
        ]
        down_parts.append(lax.ppermute(output_down_factor, ("tp", "rep"), pairs))
    down_rows = jnp.roll(jnp.stack(down_parts[::-1]), row_block + 1, axis=0)
    down_rows = down_rows.reshape(group_columns, -1)

    query_part = jnp.dot(tokens, query_matrix, preferred_element_type=jnp.float32)
    keyval_part = jnp.dot(tokens, key_value_weight, preferred_element_type=jnp.float32)
    rank_portion = jnp.dot(tokens, adapter_down_factors, preferred_element_type=jnp.float32)
    arranged = by_key_head(jnp.concatenate([query_part, keyval_part], axis=1), head_size)
    arranged = arranged.reshape(KEY_HEADS * blocks, row_count, block_cols)
    rank_blocks = jnp.broadcast_to(
        rank_portion.reshape(1, blocks, row_count, 3 * rank_width),
        (KEY_HEADS, blocks, row_count, 3 * rank_width),
    )
    rank_blocks = rank_blocks.reshape(KEY_HEADS * blocks, row_count, 3 * rank_width)
    partials = jnp.concatenate([arranged, rank_blocks], axis=2)
    partials = lax.all_to_all(partials, ("tp", "rep"), split_axis=0, concat_axis=0, tiled=True)
    combined = jnp.sum(partials, axis=0)
    rank_row_block = combined[:, block_cols:].astype(jnp.bfloat16)
    low_rank_term = jnp.concatenate(
        [
            jnp.dot(
                rank_row_block[:, :rank_width],
                up_factor[:, :group_columns],
                preferred_element_type=jnp.float32,
            ),
            jnp.dot(
                rank_row_block[:, rank_width : 2 * rank_width],
                up_factor[:, group_columns : group_columns + head_size],
                preferred_element_type=jnp.float32,
            ),
            jnp.dot(
                rank_row_block[:, 2 * rank_width :],
                up_factor[:, group_columns + head_size :],
                preferred_element_type=jnp.float32,
            ),
        ],
        axis=1,
    )
    block_total_sum = combined[:, :block_cols] + adapter_scale * low_rank_term
    query_block = block_total_sum[:, :group_columns].reshape(row_count, group_heads, head_size)
    key_new = block_total_sum[:, group_columns : group_columns + head_size]
    value_new = block_total_sum[:, group_columns + head_size :]
    my_positions = lax.dynamic_slice_in_dim(positions, row_block * row_count, row_count)
    my_lengths = lax.dynamic_slice_in_dim(lengths, row_block * row_count, row_count)
    angles = rope_angles(my_positions, head_size)
    query_rot = rotate(query_block, angles).astype(jnp.bfloat16)
    fresh_key = rotate(key_new[:, None, :], angles)[:, 0, :].astype(jnp.bfloat16)
    fresh_value = value_new.astype(jnp.bfloat16)
    mixture = attend(
        query_rot, fresh_key, fresh_value, rotated_key_cache, cached_value_rows, my_lengths
    )
    mixture = mixture.reshape(row_count, group_columns)

    low_part = jnp.dot(mixture, down_rows, preferred_element_type=jnp.float32)
    low_head = lax.reduce_precision(low_part, exponent_bits=8, mantissa_bits=7)
    message = jnp.concatenate(
        [mixture, low_head.astype(jnp.bfloat16), (low_part - low_head).astype(jnp.bfloat16)], axis=1
    )
    gathered = gather_direct(message[None], devices, dev_index)
    gathered = gathered.reshape(KEY_HEADS, blocks * row_count, -1)
    mixed_all = gathered[:, :, :group_columns].transpose(1, 0, 2).reshape(batch_rows, query_columns)
    low_terms = gathered[:, :, group_columns:].astype(jnp.float32)
    low_terms = jnp.sum(low_terms, axis=0)
    low_rank_output = low_terms[:, :rank_width] + low_terms[:, rank_width:]
    final_output = jnp.dot(mixed_all, output_matrix, preferred_element_type=jnp.float32)
    final_output = final_output + adapter_scale * jnp.dot(
        low_rank_output.astype(jnp.bfloat16), output_up_factor, preferred_element_type=jnp.float32
    )
    return (final_output.astype(jnp.bfloat16), fresh_key, fresh_value)


def solution(mesh):
    return jax.shard_map(
        per_device,
        mesh=mesh,
        in_specs=(
            P("groups", ("tp", "rep")),
            P(("tp", "rep"), None),
            P(("tp", "rep"), None),
            P(None, ("tp", "rep")),
            P(("tp", "rep"), None),
            P("tp", None),
            P(("tp", "rep"), None),
            P(None, ("tp", "rep")),
            P(("groups", "tp", "rep"), None, None),
            P(("groups", "tp", "rep"), None, None),
            P("groups"),
            P("groups"),
        ),
        out_specs=(
            P("groups", ("tp", "rep")),
            P(("groups", "tp", "rep"), None),
            P(("groups", "tp", "rep"), None),
        ),
        check_vma=False,
    )
```

```python
import math

import jax
import jax.numpy as jnp
from jax import lax
from jax.sharding import PartitionSpec as P

QUERY_HEADS = 128
KEY_HEADS = 8


adapter_scale = 2.0
rope_base = 500000.0


def rope_angles(positions, head_size):
    half_size = head_size // 2
    frequency = jnp.power(rope_base, -2.0 * jnp.arange(half_size, dtype=jnp.float32) / head_size)
    return positions.astype(jnp.float32)[:, None] * frequency[None, :]


def rotate(field, angles):
    half_size = field.shape[-1] // 2
    cosine = jnp.cos(angles)[:, None, :]
    sine_part = jnp.sin(angles)[:, None, :]
    former = field[..., :half_size]
    latter = field[..., half_size:]
    return jnp.concatenate(
        [former * cosine - latter * sine_part, latter * cosine + former * sine_part], axis=-1
    )


def attend(queries, new_key, new_value, key_rows, value_rows, lengths):
    scale_factor = 1.0 / math.sqrt(queries.shape[-1])
    scores = (
        jnp.einsum("ngd,ncd->ngc", queries, key_rows, preferred_element_type=jnp.float32)
        * scale_factor
    )
    own_score = (
        jnp.einsum("ngd,nd->ng", queries, new_key, preferred_element_type=jnp.float32)
        * scale_factor
    )
    in_range = (
        jnp.arange(key_rows.shape[1], dtype=jnp.int32)[None, None, :] < lengths[:, None, None]
    )
    scores = jnp.where(in_range, scores, -jnp.inf)
    highest = jnp.maximum(jnp.max(scores, axis=-1), own_score)
    weights = jnp.exp(scores - highest[..., None])
    own_weight = jnp.exp(own_score - highest)
    denominator = jnp.sum(weights, axis=-1) + own_weight
    prob_weights = (weights / denominator[..., None]).astype(jnp.bfloat16)
    own_prob = (own_weight / denominator).astype(jnp.bfloat16)
    mixture = jnp.einsum(
        "ngc,ncd->ngd", prob_weights, value_rows, preferred_element_type=jnp.float32
    )
    mixture = (
        mixture
        + own_prob.astype(jnp.float32)[..., None] * new_value.astype(jnp.float32)[:, None, :]
    )
    return mixture.astype(jnp.bfloat16)


def by_key_head(columns, head_size):
    rows = columns.shape[0]
    query_columns = QUERY_HEADS * head_size
    key_columns = KEY_HEADS * head_size
    query = columns[:, :query_columns].reshape(rows, KEY_HEADS, -1)
    key = columns[:, query_columns : query_columns + key_columns].reshape(rows, KEY_HEADS, -1)
    value = columns[:, query_columns + key_columns :].reshape(rows, KEY_HEADS, -1)
    return jnp.concatenate([query, key, value], axis=-1).transpose(1, 0, 2)


def to_all(value, devices):
    copies = jnp.broadcast_to(value, (devices,) + value.shape[1:])
    return lax.all_to_all(copies, ("tp", "rep"), split_axis=0, concat_axis=0, tiled=True)


def per_device(
    tokens,
    query_matrix,
    key_value_weight,
    output_matrix,
    adapter_down_factors,
    adapter_up_factors,
    output_down_factor,
    output_up_factor,
    rotated_key_cache,
    cached_value_rows,
    lengths,
    positions,
):
    tp_count = lax.axis_size("tp")
    rep_count = lax.axis_size("rep")
    devices = tp_count * rep_count
    dev_index = lax.axis_index("tp") * rep_count + lax.axis_index("rep")
    head_size = rotated_key_cache.shape[2]
    row_count = rotated_key_cache.shape[0]
    batch_rows = tokens.shape[0]
    group_heads = QUERY_HEADS // KEY_HEADS
    blocks = devices // KEY_HEADS
    row_block = dev_index % blocks
    rank_width = adapter_down_factors.shape[1] // 3
    query_columns = QUERY_HEADS * head_size
    key_value_columns = KEY_HEADS * head_size
    group_columns = group_heads * head_size
    block_cols = (group_heads + 2) * head_size

    rank_portion = jnp.dot(tokens, adapter_down_factors, preferred_element_type=jnp.float32)
    rank_rows = jnp.sum(to_all(rank_portion[None], devices), axis=0).astype(jnp.bfloat16)

    down_parts = [output_down_factor]
    for step in range(1, blocks):
        pairs = [
            (source, source // blocks * blocks + (source + step) % blocks)
            for source in range(devices)
        ]
        down_parts.append(lax.ppermute(output_down_factor, ("tp", "rep"), pairs))
    down_rows = jnp.roll(jnp.stack(down_parts[::-1]), row_block + 1, axis=0)
    down_rows = down_rows.reshape(group_columns, -1)

    query_part = jnp.dot(tokens, query_matrix, preferred_element_type=jnp.float32)
    keyval_part = jnp.dot(tokens, key_value_weight, preferred_element_type=jnp.float32)
    up_rows = adapter_up_factors.shape[0]
    mine = lax.dynamic_slice_in_dim(
        rank_rows.reshape(batch_rows, 3, rank_width), lax.axis_index("tp") * up_rows, up_rows, 2
    )
    edges = (0, query_columns, query_columns + key_value_columns, query_columns + 2 * key_value_columns)
    low_rank_term = jnp.concatenate(
        [
            jnp.dot(
                mine[:, i], adapter_up_factors[:, edges[i] : edges[i + 1]], preferred_element_type=jnp.float32
            )
            for i in range(3)
        ],
        axis=1,
    )
    partials = jnp.concatenate([query_part, keyval_part], axis=1)
    partials = partials + (adapter_scale / rep_count) * low_rank_term
    partials = by_key_head(partials, head_size)
    partials = partials.reshape(KEY_HEADS * blocks, row_count, block_cols)
    partials = lax.all_to_all(partials, ("tp", "rep"), split_axis=0, concat_axis=0, tiled=True)
    block_total_sum = jnp.sum(partials, axis=0)
    query_block = block_total_sum[:, :group_columns].reshape(row_count, group_heads, head_size)
    key_new = block_total_sum[:, group_columns : group_columns + head_size]
    value_new = block_total_sum[:, group_columns + head_size :]
    my_positions = lax.dynamic_slice_in_dim(positions, row_block * row_count, row_count)
    my_lengths = lax.dynamic_slice_in_dim(lengths, row_block * row_count, row_count)
    angles = rope_angles(my_positions, head_size)
    query_rot = rotate(query_block, angles).astype(jnp.bfloat16)
    fresh_key = rotate(key_new[:, None, :], angles)[:, 0, :].astype(jnp.bfloat16)
    fresh_value = value_new.astype(jnp.bfloat16)
    mixture = attend(
        query_rot, fresh_key, fresh_value, rotated_key_cache, cached_value_rows, my_lengths
    )
    mixture = mixture.reshape(row_count, group_columns)

    low_part = jnp.dot(mixture, down_rows, preferred_element_type=jnp.float32)
    low_head = lax.reduce_precision(low_part, exponent_bits=8, mantissa_bits=7)
    message = jnp.concatenate(
        [mixture, low_head.astype(jnp.bfloat16), (low_part - low_head).astype(jnp.bfloat16)], axis=1
    )
    gathered = to_all(message[None], devices)
    gathered = gathered.reshape(KEY_HEADS, blocks * row_count, -1)
    mixed_all = gathered[:, :, :group_columns].transpose(1, 0, 2).reshape(batch_rows, query_columns)
    low_terms = gathered[:, :, group_columns:].astype(jnp.float32)
    low_terms = jnp.sum(low_terms, axis=0)
    low_rank_output = low_terms[:, :rank_width] + low_terms[:, rank_width:]
    final_output = jnp.dot(mixed_all, output_matrix, preferred_element_type=jnp.float32)
    final_output = final_output + adapter_scale * jnp.dot(
        low_rank_output.astype(jnp.bfloat16), output_up_factor, preferred_element_type=jnp.float32
    )
    return (final_output.astype(jnp.bfloat16), fresh_key, fresh_value)


def solution(mesh):
    return jax.shard_map(
        per_device,
        mesh=mesh,
        in_specs=(
            P("groups", ("tp", "rep")),
            P(("tp", "rep"), None),
            P(("tp", "rep"), None),
            P(None, ("tp", "rep")),
            P(("tp", "rep"), None),
            P("tp", None),
            P(("tp", "rep"), None),
            P(None, ("tp", "rep")),
            P(("groups", "tp", "rep"), None, None),
            P(("groups", "tp", "rep"), None, None),
            P("groups"),
            P("groups"),
        ),
        out_specs=(
            P("groups", ("tp", "rep")),
            P(("groups", "tp", "rep"), None),
            P(("groups", "tp", "rep"), None),
        ),
        check_vma=False,
    )
```
